256 devices in a mesh: expert: 64 (over z_lo, x, y, core), tensor: 4 (over z_hi).
Axes of the slice: x: 4, y: 4, z: 8 (z_hi: 4, z_lo: 2; z = z_hi * 2 + z_lo), core: 2. Of those that a mesh axis runs over, the one named last changes fastest.
Arguments:
- tokens: bfloat16 [8192, 7168], P('expert', 'tensor'), may hold values from -6 to 6
- route: int32 [8192, 2], P('expert'), may hold values from 0 to 31, all different within a row; in each aligned block of 128 rows (0 to 127, 128 to 255, ...) at most 12 rows name the same one
- probs: float32 [8192, 2], P('expert'), may hold values from 0.2 to 1
- cotangent: bfloat16 [8192, 7168], P('expert', 'tensor'), may hold values from -6 to 6
- gate_weight: bfloat16 [64, 7168, 512], P('expert', 'tensor'), may hold values from -0.0625 to 0.0625
- up_weight: bfloat16 [64, 7168, 512], P('expert', 'tensor'), may hold values from -0.0625 to 0.0625
- down_weight: bfloat16 [64, 512, 7168], P('expert', None, 'tensor'), may hold values from -0.1875 to 0.1875
Outputs:
- moe_out: bfloat16 [8192, 7168], P('expert', 'tensor')
- grad_probs: float32 [8192, 2], P('expert')
- grad_tokens: bfloat16 [8192, 7168], P('expert', 'tensor')
- grad_gate: bfloat16 [64, 7168, 512], P('expert', 'tensor')
- grad_up: bfloat16 [64, 7168, 512], P('expert', 'tensor')
- grad_down: bfloat16 [64, 512, 7168], P('expert', None, 'tensor')
The draws below stay inside these ranges and needn't reach their ends.
Inputs may be any that keep to these rules, and one draw needn't show every extreme that they name: `route`: within each aligned block of 128 rows (the rows of one device) no expert is named more than 12 times, and in some blocks some expert exactly 12 times; the 2 entries of a row differ and every expert is named somewhere.
All inputs are finite; a program needn't handle non-finite values.
Results may differ from the reference program's by a relative error of at most 0.0064.
Values may be sent and summed in bfloat16 or wider, within the bound.
No kernel may reach another device: no remote copies, remote signals or barrier semaphores. Data moves between devices by JAX's collectives and lax.ppermute only.
A program may use at most 128 MiB of HBM per device.

```python
import math
import jax
import jax.numpy as jnp
import numpy as np
from jax import lax

D = 7168
FF = 1024
TOPK = 2
TOK_DEV = 128
EXPERTS = 32
MOST = 12
TOKENS = 8192
N_EXPERT = 64


def block_scale(key, shape, cuts, least, top_value):
    loudness = 1.0
    for dim, shards_of in cuts:
        heights = jax.random.uniform(jax.random.fold_in(jax.random.fold_in(key, 6), dim), (shards_of,), jnp.float32, least / len(cuts), top_value / len(cuts))
        loudness = loudness * jnp.repeat(jnp.exp(heights), shape[dim] // shards_of).reshape((-1,) + (1,) * (len(shape) - 1 - dim))
    return loudness


def shared_out(own_key, own, number, rows, amount, top, most, slope):
    order = jax.random.permutation(own_key, amount)
    heavy_load, common = shares(amount, rows * top, most, slope, True), shares(amount, rows * top, most, slope, False)
    places = jnp.arange(amount)

    def named(lengths, offset_by):
        used = int((lengths > 0).sum())
        fixed = max(1, used // 4)
        moved = fixed + (places - fixed + offset_by * (used - fixed)) % max(1, amount - fixed)
        return jnp.zeros((amount,), jnp.int32).at[order[jnp.where(places < fixed, places, moved)]].set(jnp.asarray(lengths, jnp.int32))

    lengths = jnp.where(number % 4 == 0, named(heavy_load, number // 4), named(common, number - number // 4 - 1))
    mixed = jax.random.permutation(jax.random.fold_in(own, 3), amount)
    donor, receiver = mixed[0:amount // 2 * 2:2], mixed[1:amount // 2 * 2:2]
    margin = jnp.minimum(lengths[donor] - 1, most - lengths[receiver]) // 2
    margin = jnp.where((donor == order[0]) | (receiver == order[0]) | (lengths[receiver] == 0), 0, jnp.maximum(margin, 0))
    moved = jax.random.randint(jax.random.fold_in(own, 4), (amount // 2,), 0, 1 << 20) % (margin + 1)
    lengths = lengths.at[donor].add(-moved).at[receiver].add(moved)
    items = jnp.searchsorted(jnp.cumsum(lengths), jnp.arange(rows * top), side="right").astype(jnp.int32)
    table = items.reshape(top, rows).T
    table = table[jax.random.permutation(jax.random.fold_in(own, 1), rows)]
    offset_by = jax.random.randint(jax.random.fold_in(own, 2), (rows, 1), 0, top)
    return jnp.take_along_axis(table, (jnp.arange(top)[None, :] + offset_by) % top, axis=1)


def shares(count, total, reach, slope, full):
    loads = [(1 << 20) // math.isqrt(standing ** slope) + 1 for standing in range(1, count + 1)]
    largest = reach if full else min(reach, max(-(-total // count), total * loads[0] // sum(loads)))
    least = 1 if total - largest >= count - 1 else 0
    counts, surplus = [largest] + [least] * (count - 1), total - largest - least * (count - 1)
    while surplus > 0:
        free = [i for i in range(1, count) if counts[i] < largest] or [i for i in range(1, count) if counts[i] < reach]
        whole, left = sum([loads[i] for i in free]), surplus
        for i in free:
            extra = min(reach - counts[i], max(1, left * loads[i] // whole), surplus)
            counts[i] = counts[i] + extra
            surplus = surplus - extra
    return np.array(counts)


def bell_draw(key, shape, spread, most, shards=(), kind=jnp.bfloat16):
    entries = jax.random.normal(key, shape, jnp.float32) * spread
    if len(shards) > 0:
        entries = block_scale(key, shape, shards, -0.22, 0.18) * entries
    return jnp.clip(entries, min=-most, max=most).astype(kind)


def setup_inputs(seed: int = 0) -> dict:
    seeds = jax.random.split(jax.random.key(seed), 8)
    tokens = bell_draw(seeds[0], (TOKENS, D), 1.0, 6.0, ((0, 64), (1, 4)))
    route_keys = jax.random.split(jax.random.fold_in(seeds[1], 1), TOKENS // TOK_DEV)
    route_turns = jax.random.permutation(jax.random.fold_in(seeds[1], 3), TOKENS // TOK_DEV)
    route = jax.vmap(lambda own, number: shared_out(jax.random.fold_in(seeds[1], 2), own, number, TOK_DEV, EXPERTS, TOPK, MOST, 2))(route_keys, route_turns).reshape((TOKENS, TOPK))
    probs = jnp.clip(0.2 + 0.8 * jax.random.uniform(seeds[2], (TOKENS, TOPK), jnp.float32) ** block_scale(seeds[2], (TOKENS, TOPK), ((0, 64),), -0.2, 0.2), 0.2, 1.0)
    cotangent = bell_draw(seeds[3], (TOKENS, D), 1.0, 6.0, ((0, 64), (1, 4)))
    gate_weight = bell_draw(seeds[4], (N_EXPERT, D, FF // 2), D ** -0.5, 0.0625, ((0, 64), (1, 4)))
    up_weight = bell_draw(seeds[5], (N_EXPERT, D, FF // 2), D ** -0.5, 0.0625, ((0, 64), (1, 4)))
    down_weight = bell_draw(seeds[6], (N_EXPERT, FF // 2, D), FF ** -0.5, 0.1875, ((0, 64), (2, 4)))
    return {"tokens": tokens, "route": route, "probs": probs, "cotangent": cotangent, "gate_weight": gate_weight, "up_weight": up_weight, "down_weight": down_weight}


def slot_ranks(route):
    blocks = route.reshape(N_EXPERT, TOK_DEV * TOPK)
    labels = jnp.arange(EXPERTS, dtype=jnp.int32)
    onehot = (blocks[:, :, None] == labels[None, None, :]).astype(jnp.int32)
    before = jnp.cumsum(onehot, axis=1) - onehot
    return jnp.sum(before * onehot, axis=2).reshape(TOKENS, TOPK).astype(jnp.int32)


def reference(tokens, route, probs, cotangent, gate_weight, up_weight, down_weight):
    ranks = slot_ranks(route)
    token_ids = jnp.broadcast_to(jnp.arange(TOKENS, dtype=jnp.int32)[:, None], (TOKENS, TOPK))
    choice_ids = jnp.broadcast_to(jnp.arange(TOPK, dtype=jnp.int32)[None, :], (TOKENS, TOPK))
    position = ((token_ids // TOK_DEV) * MOST + ranks).astype(jnp.int32)
    slot_count = N_EXPERT * MOST
    row_table = jnp.full((EXPERTS, slot_count), TOKENS, jnp.int32).at[route, position].set(token_ids)
    pick_table = jnp.zeros((EXPERTS, slot_count), jnp.int32).at[route, position].set(choice_ids)
    prob_table = jnp.zeros((EXPERTS, slot_count), jnp.float32).at[route, position].set(probs)
    tok_padded = jnp.concatenate([tokens, jnp.zeros((1, D), tokens.dtype)], axis=0)
    cot_padded = jnp.concatenate([cotangent.astype(jnp.float32), jnp.zeros((1, D), jnp.float32)], axis=0)
    half_width = FF // 2

    def expert_step(totals, expert_id):
        out_acc, in_acc, prob_acc = totals
        row_ids = row_table[expert_id]
        pick_ids = pick_table[expert_id]
        weights_slot = prob_table[expert_id]
        first_half = 2 * expert_id
        second_half = first_half + 1
        expert_in = tok_padded[row_ids]
        w_gate = jnp.concatenate([gate_weight[first_half], gate_weight[second_half]], axis=1)
        w_up = jnp.concatenate([up_weight[first_half], up_weight[second_half]], axis=1)
        w_down = jnp.concatenate([down_weight[first_half], down_weight[second_half]], axis=0)
        gate_val = jnp.dot(expert_in, w_gate, preferred_element_type=jnp.float32)
        up_val = jnp.dot(expert_in, w_up, preferred_element_type=jnp.float32)
        hidden = (jax.nn.silu(gate_val) * up_val).astype(jnp.bfloat16)
        part_first = jnp.dot(hidden[:, :half_width], down_weight[first_half], preferred_element_type=jnp.float32).astype(jnp.bfloat16)
        part_second = jnp.dot(hidden[:, half_width:], down_weight[second_half], preferred_element_type=jnp.float32).astype(jnp.bfloat16)
        picked = part_first.astype(jnp.float32) + part_second.astype(jnp.float32)
        cot_rows = cot_padded[row_ids]
        out_acc = out_acc.at[row_ids].add(weights_slot[:, None] * picked)
        prob_acc = prob_acc.at[row_ids, pick_ids].add(jnp.sum(picked * cot_rows, axis=1))
        expert_cot = (weights_slot[:, None] * cot_rows).astype(jnp.bfloat16)
        hidden_cot = jnp.dot(expert_cot, w_down.T, preferred_element_type=jnp.float32)
        gate_sig = jax.nn.sigmoid(gate_val)
        gate_cot = (hidden_cot * up_val * gate_sig * (1.0 + gate_val * (1.0 - gate_sig))).astype(jnp.bfloat16)
        up_cot = (hidden_cot * gate_val * gate_sig).astype(jnp.bfloat16)
        in_first = (jnp.dot(gate_cot[:, :half_width], gate_weight[first_half].T, preferred_element_type=jnp.float32)
                    + jnp.dot(up_cot[:, :half_width], up_weight[first_half].T, preferred_element_type=jnp.float32)).astype(jnp.bfloat16)
        in_second = (jnp.dot(gate_cot[:, half_width:], gate_weight[second_half].T, preferred_element_type=jnp.float32)
                     + jnp.dot(up_cot[:, half_width:], up_weight[second_half].T, preferred_element_type=jnp.float32)).astype(jnp.bfloat16)
        in_acc = in_acc.at[row_ids].add(in_first.astype(jnp.float32) + in_second.astype(jnp.float32))
        grad_gate = jnp.dot(expert_in.T, gate_cot, preferred_element_type=jnp.float32).astype(jnp.bfloat16)
        grad_up = jnp.dot(expert_in.T, up_cot, preferred_element_type=jnp.float32).astype(jnp.bfloat16)
        grad_down = jnp.dot(hidden.T, expert_cot, preferred_element_type=jnp.float32).astype(jnp.bfloat16)
        return (out_acc, in_acc, prob_acc), (grad_gate, grad_up, grad_down)

    start = (jnp.zeros((TOKENS + 1, D), jnp.float32), jnp.zeros((TOKENS + 1, D), jnp.float32),
             jnp.zeros((TOKENS + 1, TOPK), jnp.float32))
    totals, grads = lax.scan(expert_step, start, jnp.arange(EXPERTS, dtype=jnp.int32))
    out_acc, in_acc, prob_acc = totals
    grad_gate, grad_up, grad_down = grads
    grad_gate = grad_gate.reshape(EXPERTS, D, 2, half_width).transpose(0, 2, 1, 3).reshape(N_EXPERT, D, half_width)
    grad_up = grad_up.reshape(EXPERTS, D, 2, half_width).transpose(0, 2, 1, 3).reshape(N_EXPERT, D, half_width)
    grad_down = grad_down.reshape(N_EXPERT, half_width, D)
    moe_out = out_acc[:TOKENS].astype(jnp.bfloat16)
    grad_tokens = in_acc[:TOKENS].astype(jnp.bfloat16)
    return (moe_out, prob_acc[:TOKENS], grad_tokens, grad_gate, grad_up, grad_down)
```

```python
import jax
import jax.numpy as jnp
from jax import lax
from jax.sharding import Mesh, PartitionSpec as P

BF = jnp.bfloat16
F32 = jnp.float32
PAIR = [(0, 1), (1, 0)]
EDGE_A = [(0, 1), (1, 0), (2, 3), (3, 2)]
EDGE_B = [(0, 3), (3, 0), (1, 2), (2, 1)]


def swap(value, axis):
    return lax.ppermute(value, axis, PAIR)


def cross(value, edge):
    return lax.ppermute(value, "tensor", edge)


def pick_block(value, index):
    return lax.dynamic_index_in_dim(value, index, 0, keepdims=False)


def scatter_sum(value, first_bit, second_bit, first_edge, second_edge):
    rows, width = value.shape
    blocks = value.reshape(2, 2, rows // 4, width)
    away = pick_block(blocks, 1 - first_bit).astype(BF)
    mine = pick_block(blocks, first_bit) + cross(away, first_edge).astype(F32)
    away = pick_block(mine, 1 - second_bit).astype(BF)
    return pick_block(mine, second_bit) + cross(away, second_edge).astype(F32)


def in_order(mine, other, bit):
    return jnp.where(
        bit == 0, jnp.concatenate([mine, other], 0), jnp.concatenate([other, mine], 0)
    )


def gather_rows(value, first_bit, second_bit, first_edge, second_edge):
    pair = in_order(value, cross(value, second_edge), second_bit)
    return in_order(pair, cross(pair, first_edge), first_bit)


def dot(a, b, dims):
    return lax.dot_general(a, b, (dims, ((), ())), preferred_element_type=F32)


NN = ((1,), (0,))
NT = ((1,), (1,))
TN = ((0,), (0,))


def on_device(tokens, route, probs, cotangent, gate_weight, up_weight, down_weight):
    tok_rows, quarter = tokens.shape
    top_count = route.shape[1]
    planes = lax.axis_size("z")
    chips = lax.axis_size("x") * lax.axis_size("y")
    experts = planes * chips
    capacity = 3 * tok_rows * top_count // (2 * experts)
    slots = chips * planes * capacity
    z_index = lax.axis_index("z")
    t_index = lax.axis_index("tensor")
    bit_b = t_index // 2
    bit_a = (t_index + 1) // 2 % 2
    w_gate, w_up, w_down = gate_weight[0], up_weight[0], down_weight[0]

    tok_peer = swap(tokens, "z")
    cot_peer = swap(cotangent, "z")

    flat_route = route.reshape(tok_rows * top_count)
    onehot = flat_route[:, None] == jnp.arange(experts, dtype=jnp.int32)[None, :]
    picks = tok_rows * top_count
    earlier = (jnp.arange(picks)[:, None] > jnp.arange(picks)[None, :]).astype(BF)
    before = dot(earlier, onehot.astype(BF), NN)
    rank = jnp.sum(jnp.where(onehot, before, 0.0), axis=1).astype(jnp.int32)
    slot = flat_route // chips * slots + flat_route % chips * (planes * capacity) + rank
    packed = jnp.concatenate(
        [slot.reshape(tok_rows, top_count).T.astype(F32), probs.T], 0
    )
    packed_peer = swap(packed, "z")

    def seen(pack, place):
        local = pack[:top_count].astype(jnp.int32) - z_index * slots + place * capacity
        inside = (pack[:top_count] >= (z_index * slots).astype(F32)) & (
            pack[:top_count] < ((z_index + 1) * slots).astype(F32)
        )
        return jnp.where(inside, local, -1)

    local = jnp.concatenate([seen(packed, 0), seen(packed_peer, 1)], 1)
    prob = jnp.concatenate([packed[top_count:], packed_peer[top_count:]], 1)
    selector = local[:, None, :] == jnp.arange(slots, dtype=jnp.int32)[None, :, None]
    assign = jnp.any(selector, axis=0).astype(BF)
    slot_prob = jnp.sum(jnp.where(selector, prob[:, None, :], 0.0), axis=(0, 2))

    def dispatch(rows):
        sent = lax.all_to_all(
            rows.reshape(chips, planes * capacity, quarter),
            ("x", "y"),
            split_axis=0,
            concat_axis=0,
            tiled=True,
        ).reshape(slots, quarter)
        return sent, swap(sent, "core")

    tok_all = jnp.concatenate([tokens, tok_peer], 0)
    cot_all = jnp.concatenate([cotangent, cot_peer], 0)
    in_mine, in_other = dispatch(dot(assign, tok_all, NN).astype(BF))
    cot_mine, cot_other = dispatch((slot_prob[:, None] * dot(assign, cot_all, NN)).astype(BF))

    first = (bit_a, bit_b, EDGE_A, EDGE_B)
    second = (bit_b, bit_a, EDGE_B, EDGE_A)

    def gate_up(rows):
        return jnp.concatenate([dot(rows, w_gate, NN), dot(rows, w_up, NN)], 1)

    gu_mine = scatter_sum(gate_up(in_mine), *first)
    gu_other = scatter_sum(gate_up(in_other), *second)
    hc_mine = scatter_sum(dot(cot_mine, w_down, NT), *first)
    hc_other = scatter_sum(dot(cot_other, w_down, NT), *second)
    half = w_gate.shape[1]

    def forward(gu):
        gate, up = gu[:, :half], gu[:, half:]
        return (jax.nn.silu(gate) * up).astype(BF)

    def backward(gu, hc):
        gate, up = gu[:, :half], gu[:, half:]
        sig = jax.nn.sigmoid(gate)
        gate_cot = (hc * up * sig * (1.0 + gate * (1.0 - sig))).astype(BF)
        up_cot = (hc * gate * sig).astype(BF)
        return jnp.concatenate([gate_cot, up_cot], 1)

    hid_mine = gather_rows(forward(gu_mine), *first)
    hid_other = gather_rows(forward(gu_other), *second)
    gc_mine = gather_rows(backward(gu_mine, hc_mine), *first)
    gc_other = gather_rows(backward(gu_other, hc_other), *second)

    def send_back(product, mine, other):
        theirs = swap(product(other).astype(BF), "core")
        rows = (product(mine) + theirs.astype(F32)).astype(BF)
        return lax.all_to_all(
            rows.reshape(chips, planes * capacity, quarter),
            ("x", "y"),
            split_axis=0,
            concat_axis=0,
            tiled=True,
        ).reshape(slots, quarter)

    def out_rows(rows):
        return dot(rows, w_down, NN)

    def in_rows(rows):
        return dot(rows[:, :half], w_gate, NT) + dot(rows[:, half:], w_up, NT)

    returned = send_back(out_rows, hid_mine, hid_other)
    returned_in = send_back(in_rows, gc_mine, gc_other)

    picked = [dot(selector[k].astype(BF), returned, TN) for k in range(top_count)]
    partial = sum(prob[k][:, None] * picked[k] for k in range(top_count))
    cot_float = cot_all.astype(F32)
    grad_p = jnp.stack([jnp.sum(picked[k] * cot_float, axis=1) for k in range(top_count)])
    moe_out = (partial[:tok_rows] + swap(partial[tok_rows:].astype(BF), "z").astype(F32)).astype(BF)
    grad_p = grad_p[:, :tok_rows] + swap(grad_p[:, tok_rows:], "z")
    grad_p = grad_p + cross(grad_p, EDGE_A)
    grad_p = grad_p + cross(grad_p, EDGE_B)

    tok_part = dot(assign, returned_in, TN)
    grad_tokens = (tok_part[:tok_rows] + swap(tok_part[tok_rows:].astype(BF), "z").astype(F32)).astype(BF)

    rows_in = jnp.concatenate([in_mine, in_other], 0)
    rows_cot = jnp.concatenate([cot_mine, cot_other], 0)
    hidden = jnp.concatenate([hid_mine, hid_other], 0)
    cots = jnp.concatenate([gc_mine, gc_other], 0)
    grad_gate = dot(rows_in, cots[:, :half], TN).astype(BF)
    grad_up = dot(rows_in, cots[:, half:], TN).astype(BF)
    grad_down = dot(hidden, rows_cot, TN).astype(BF)
    return (moe_out, grad_p.T, grad_tokens, grad_gate[None], grad_up[None], grad_down[None])


def solution(mesh):
    lanes = ("z", "x", "y", "core")
    fine = Mesh(mesh.devices.reshape(2, 4, 4, 2, 4), lanes + ("tensor",))
    placed = (
        P(lanes, "tensor"),
        P(lanes, None),
        P(lanes, None),
        P(lanes, "tensor"),
        P(lanes, "tensor", None),
        P(lanes, "tensor", None),
        P(lanes, None, "tensor"),
    )
    return jax.shard_map(
        on_device,
        mesh=fine,
        in_specs=placed,
        out_specs=(
            P(lanes, "tensor"),
            P(lanes, None),
            P(lanes, "tensor"),
            P(lanes, "tensor", None),
            P(lanes, "tensor", None),
            P(lanes, None, "tensor"),
        ),
        check_vma=False,
    )
```

```python
import jax
import jax.numpy as jnp
from jax import lax
from jax.experimental import pallas as pl
from jax.experimental.pallas import tpu as pltpu
from jax.sharding import Mesh, PartitionSpec as P

BF = jnp.bfloat16
F32 = jnp.float32
PAIR = [(0, 1), (1, 0)]
EDGE_A = [(0, 1), (1, 0), (2, 3), (3, 2)]
EDGE_B = [(0, 3), (3, 0), (1, 2), (2, 1)]


def swap(value, axis):
    return lax.ppermute(value, axis, PAIR)


FIRST = [(i, j) for i, j in EDGE_A] + [(4 + i, 4 + j) for i, j in EDGE_B]
SECOND = [(i, j) for i, j in EDGE_B] + [(4 + i, 4 + j) for i, j in EDGE_A]


def cross(value, step):
    return lax.ppermute(value, ("core", "tensor"), step)


def tie(value, after):
    return lax.optimization_barrier((value, after))[0]


def dot(a, b, dims):
    return lax.dot_general(a, b, (dims, ((), ())), preferred_element_type=F32)


NN = ((1,), (0,))
NT = ((1,), (1,))
TN = ((0,), (0,))


def local_call(kernel, out_shape, code, *args):
    vmem = pl.BlockSpec(memory_space=pltpu.VMEM)
    return pl.pallas_call(
        kernel,
        in_specs=[pl.BlockSpec(memory_space=pltpu.SMEM)] + [vmem] * len(args),
        out_specs=jax.tree.map(lambda _: vmem, out_shape),
        out_shape=out_shape,
        compiler_params=pltpu.CompilerParams(vmem_limit_bytes=20 * 1024 * 1024),
        cost_estimate=pl.CostEstimate(flops=1000, bytes_accessed=1000, transcendentals=0),
    )(code, *args)


def shuffled(value, bit):
    half = value.shape[0] // 2
    return [(part ^ bit, value[part * half : (part + 1) * half]) for part in range(2)]


def first_kernel(product, count, code, mine, top, bottom, *refs):
    weights, (keep, away, rel) = refs[:count], refs[count:]

    def half_of_rows(step, rows):
        for place, part in shuffled(rows, code[1]):
            rel[step, place] = part
        column = 0
        for weight in weights:
            value = product(rows, weight[...])
            width = value.shape[1]
            for place, part in shuffled(value, code[1]):

                @pl.when(step == 0)
                def _():
                    keep[place, :, column : column + width] = part

                @pl.when(step == 1)
                def _():
                    away[place, :, column : column + width] = part.astype(BF)

            column += width

    @pl.loop(0, 2)
    def _(step):
        other = jnp.concatenate([top[...], bottom[...]], 0)
        half_of_rows(step, jnp.where((step ^ code[0]) == 0, mine[...], other))


def first_products(product, code, mine, other, weights, width):
    rows, quarter = mine.shape
    block = rows // 2
    return local_call(
        lambda *refs: first_kernel(product, len(weights), *refs),
        [
            jax.ShapeDtypeStruct((2, block, width), F32),
            jax.ShapeDtypeStruct((2, block, width), BF),
            jax.ShapeDtypeStruct((2, 2, block, quarter), BF),
        ],
        code,
        mine,
        *other,
        *weights,
    )


def finish(value, theirs, outs):
    half = value.shape[0] // 2
    for j in range(2):
        part = value[j * half : (j + 1) * half]
        if theirs:
            outs[0][j * half : (j + 1) * half, :] = (part + theirs[j][...].astype(F32)).astype(BF)
        else:
            outs[j][...] = part.astype(BF)


def out_rows_kernel(side, code, hidden, w_down, *refs):
    theirs, outs = refs[:2], refs[2:]
    if side == 1:
        theirs, outs = (), refs
    parts = [hidden[2 * (side ^ code[0]) + (j ^ code[1])] for j in range(2)]
    value = dot(jnp.concatenate(parts, 0), w_down[...], NN)
    finish(value, theirs, outs)


def in_rows_kernel(side, code, near, far, w_gate, w_up, *refs):
    theirs, outs = refs[:2], refs[2:]
    if side == 1:
        theirs, outs = (), refs
    place = side ^ code[0]
    value = None
    for kind, weight in ((0, w_gate), (1, w_up)):
        pair = near[2 * place + kind], far[2 * place + kind]
        parts = [jnp.where((j ^ code[1]) == 0, *pair) for j in range(2)]
        term = dot(jnp.concatenate(parts, 0), weight[...], NT)
        value = term if value is None else value + term
    finish(value, theirs, outs)


def last_products(kernel, code, pieces, weights, quarter, theirs):
    side = 1 if theirs is None else 0
    rows = pieces[0].shape[1]
    whole_shape = jax.ShapeDtypeStruct((2 * rows, quarter), BF)
    half_shape = jax.ShapeDtypeStruct((rows, quarter), BF)
    return local_call(
        lambda *refs: kernel(side, *refs),
        [half_shape] * 2 if theirs is None else whole_shape,
        code,
        *pieces,
        *weights,
        *([] if theirs is None else theirs),
    )


def slots_kernel(chips, capacity, planes, z_ref, route_mine, route_peer, local, assign):
    tokens = route_mine.shape[0]
    slots = assign.shape[1]
    lanes = lax.broadcasted_iota(jnp.int32, (tokens, 128), 1)
    earlier = lax.broadcasted_iota(jnp.int32, (tokens, tokens), 0) > lax.broadcasted_iota(
        jnp.int32, (tokens, tokens), 1
    )
    places = lax.broadcasted_iota(jnp.int32, (tokens, slots), 1)
    for block, route in enumerate((route_mine, route_peer)):
        named = [route[:, k : k + 1] for k in range(2)]
        onehot = [(named[k] == lanes).astype(F32) for k in range(2)]
        before = dot(earlier.astype(BF), (onehot[0] + onehot[1]).astype(BF), NN)
        chosen = jnp.zeros((tokens, slots), F32)
        for k in range(2):
            rank = jnp.sum(before * onehot[k], axis=1, keepdims=True).astype(jnp.int32)
            expert = named[k] - z_ref[0] * chips
            inside = (expert >= 0) & (expert < chips)
            slot = jnp.where(inside, expert * (planes * capacity) + block * capacity + rank, -1)
            local[block * tokens : (block + 1) * tokens, k : k + 1] = slot
            chosen = chosen + (slot == places).astype(F32)
        assign[block * tokens : (block + 1) * tokens, :] = chosen.astype(BF)


def rows_kernel(_, assign, mine, peer, out):
    tokens = mine.shape[0]
    rows = dot(assign[:tokens], mine[...], TN) + dot(assign[tokens:], peer[...], TN)
    out[...] = rows.astype(BF)


def picks_of(local, k, first, last, slots):
    places = lax.broadcasted_iota(jnp.int32, (last - first, slots), 1)
    return (local[first:last, k : k + 1] == places).astype(F32).astype(BF)


def cot_rows_kernel(_, local, prob, mine, peer, out):
    tokens = mine.shape[0]
    slots = out.shape[0]
    total = None
    for block, cot in enumerate((mine, peer)):
        first, last = block * tokens, (block + 1) * tokens
        value = cot[...].astype(F32)
        for k in range(2):
            scaled = (prob[first:last, k : k + 1] * value).astype(BF)
            term = dot(picks_of(local, k, first, last, slots), scaled, TN)
            total = term if total is None else total + term
    out[...] = total.astype(BF)


def combine_kernel(_, local, prob, rows, mine, peer, out_mine, out_peer, grad_p):
    tokens = mine.shape[0]
    slots = rows.shape[0]
    for block, (cot, out) in enumerate(((mine, out_mine), (peer, out_peer))):
        first, last = block * tokens, (block + 1) * tokens
        total = None
        for k in range(2):
            picked = dot(picks_of(local, k, first, last, slots), rows[...], NN)
            term = prob[first:last, k : k + 1] * picked
            total = term if total is None else total + term
            grad = jnp.sum(picked * cot[...].astype(F32), axis=1, keepdims=True)
            grad_p[first:last, k : k + 1] = grad
        out[...] = total.astype(out.dtype)


def on_device(tokens, route, probs, cotangent, gate_weight, up_weight, down_weight):
    tok_rows, quarter = tokens.shape
    top_count = route.shape[1]
    planes = lax.axis_size("z")
    chips = lax.axis_size("x") * lax.axis_size("y")
    experts = planes * chips
    capacity = 3 * tok_rows * top_count // (2 * experts)
    slots = chips * planes * capacity
    z_index = lax.axis_index("z")
    t_index = lax.axis_index("tensor")
    bit_b = t_index // 2
    bit_a = (t_index + 1) // 2 % 2
    core = lax.axis_index("core")
    code = jnp.stack(
        [jnp.where(core == 0, bit_a, bit_b), jnp.where(core == 0, bit_b, bit_a)]
    ).astype(jnp.int32)
    w_gate, w_up, w_down = gate_weight[0], up_weight[0], down_weight[0]

    route_peer, probs_peer = swap(route, "z"), swap(probs, "z")
    tok_peer = swap(tokens, "z")
    cot_peer = swap(tie(cotangent, tok_peer), "z")
    prob = jnp.concatenate([probs, probs_peer], 0)
    local, assign = local_call(
        lambda *refs: slots_kernel(chips, capacity, planes, *refs),
        [
            jax.ShapeDtypeStruct((planes * tok_rows, top_count), jnp.int32),
            jax.ShapeDtypeStruct((planes * tok_rows, slots), BF),
        ],
        z_index.astype(jnp.int32)[None],
        route,
        route_peer,
    )
    rows_shape = jax.ShapeDtypeStruct((slots, quarter), BF)

    def exchange(rows):
        return lax.all_to_all(
            rows.reshape(chips, planes * capacity, quarter),
            ("x", "y"),
            split_axis=0,
            concat_axis=0,
            tiled=True,
        ).reshape(slots, quarter)

    def collect(sent):
        return sent, [swap(sent[: slots // 2], "core"), swap(sent[slots // 2 :], "core")]

    tok_sent = exchange(local_call(rows_kernel, rows_shape, code, assign, tokens, tok_peer))
    cot_rows = local_call(cot_rows_kernel, rows_shape, code, local, prob, cotangent, cot_peer)
    cot_sent = exchange(tie(cot_rows, tok_sent))
    in_mine, in_other = collect(tie(tok_sent, cot_rows))
    half = w_gate.shape[1]

    def nn(rows, weight):
        return dot(rows, weight, NN)

    def nt(rows, weight):
        return dot(rows, weight, NT)

    keep, away, rows_in = first_products(nn, code, in_mine, in_other, (w_gate, w_up), 2 * half)
    got = cross(away, FIRST)
    cot_mine, cot_other = collect(tie(cot_sent, away))
    keep_c, away_c, rows_cot = first_products(nt, code, cot_mine, cot_other, (w_down,), half)
    got_c = cross(away_c, FIRST)
    gate_up = keep + tie(got, away_c).astype(F32)
    got = cross(gate_up[1].astype(BF), SECOND)

    gate_up = gate_up[0] + got.astype(F32)
    gate, up = gate_up[:, :half], gate_up[:, half:]
    hidden = (jax.nn.silu(gate) * up).astype(BF)

    hidden_cot = keep_c + got_c.astype(F32)
    got = cross(jnp.stack([hidden_cot[1].astype(BF), hidden]), SECOND)
    hidden_cot = hidden_cot[0] + got[0].astype(F32)
    hidden = jnp.stack([hidden, got[1]])
    sig = jax.nn.sigmoid(gate)
    gate_cot = (hidden_cot * up * sig * (1.0 + gate * (1.0 - sig))).astype(BF)
    up_cot = (hidden_cot * gate * sig).astype(BF)

    own = jnp.stack([gate_cot, up_cot])
    hidden = jnp.concatenate([hidden, cross(hidden, FIRST)], 0)
    got = cross(own, FIRST)

    def send_back(kernel, pieces, weights, after=None):
        away = last_products(kernel, code, pieces, weights, quarter, None)
        theirs = [swap(part, "core") for part in away]
        if after is not None:
            theirs = tie(theirs, after)
        return last_products(kernel, code, pieces, weights, quarter, theirs)

    out_back = send_back(out_rows_kernel, (hidden,), (w_down,))
    returned = exchange(out_back)
    near = jnp.concatenate([own, got], 0)
    far = cross(near, SECOND)
    hidden, rows_cot = tie((hidden, rows_cot), out_back)
    grad_down = dot(hidden.reshape(2 * slots, half), rows_cot.reshape(2 * slots, quarter), TN).astype(BF)
    out_mine, out_peer, grad_p = local_call(
        combine_kernel,
        [
            jax.ShapeDtypeStruct((tok_rows, quarter), F32),
            jax.ShapeDtypeStruct((tok_rows, quarter), BF),
            jax.ShapeDtypeStruct((planes * tok_rows, top_count), F32),
        ],
        code,
        local,
        prob,
        returned,
        cotangent,
        cot_peer,
    )
    in_back = send_back(in_rows_kernel, (near, far), (w_gate, w_up), (out_peer, grad_down))
    returned_in = exchange(in_back)
    near, far, out_mine, grad_p = tie((near, far, out_mine, grad_p), in_back)

    moe_out = (out_mine + swap(out_peer, "z").astype(F32)).astype(BF)
    grad_p = grad_p.T
    grad_p = grad_p[:, :tok_rows] + swap(grad_p[:, tok_rows:], "z")
    grad_p = grad_p + cross(grad_p, FIRST)
    grad_p = grad_p + cross(grad_p, SECOND)

    tok_part = dot(assign, returned_in, NN)
    grad_tokens = (tok_part[:tok_rows] + swap(tok_part[tok_rows:].astype(BF), "z").astype(F32)).astype(BF)

    rows_in = rows_in.reshape(2 * slots, quarter)

    def all_rows(kind):
        parts = [near[kind], far[kind], near[2 + kind], far[2 + kind]]
        return jnp.concatenate(parts, 0)

    grad_gate = dot(rows_in, all_rows(0), TN).astype(BF)
    grad_up = dot(rows_in, all_rows(1), TN).astype(BF)
    return (moe_out, grad_p.T, grad_tokens, grad_gate[None], grad_up[None], grad_down[None])


def solution(mesh):
    lanes = ("z", "x", "y", "core")
    fine = Mesh(mesh.devices.reshape(2, 4, 4, 2, 4), lanes + ("tensor",))
    placed = (
        P(lanes, "tensor"),
        P(lanes, None),
        P(lanes, None),
        P(lanes, "tensor"),
        P(lanes, "tensor", None),
        P(lanes, "tensor", None),
        P(lanes, None, "tensor"),
    )
    return jax.shard_map(
        on_device,
        mesh=fine,
        in_specs=placed,
        out_specs=(
            P(lanes, "tensor"),
            P(lanes, None),
            P(lanes, "tensor"),
            P(lanes, "tensor", None),
            P(lanes, "tensor", None),
            P(lanes, None, "tensor"),
        ),
        check_vma=False,
    )
```

```python
import jax
import jax.numpy as jnp
from jax import lax
from jax.experimental import pallas as pl
from jax.experimental.pallas import tpu as pltpu
from jax.sharding import Mesh, PartitionSpec as P

BF = jnp.bfloat16
F32 = jnp.float32
PAIR = [(0, 1), (1, 0)]
EDGE_A = [(0, 1), (1, 0), (2, 3), (3, 2)]
EDGE_B = [(0, 3), (3, 0), (1, 2), (2, 1)]


def swap(value, axis):
    return lax.ppermute(value, axis, PAIR)


FIRST = [(i, j) for i, j in EDGE_A] + [(4 + i, 4 + j) for i, j in EDGE_B]
SECOND = [(i, j) for i, j in EDGE_B] + [(4 + i, 4 + j) for i, j in EDGE_A]


def cross(value, step):
    return lax.ppermute(value, ("core", "tensor"), step)


def tie(value, after):
    return lax.optimization_barrier((value, after))[0]


def dot(a, b, dims):
    return lax.dot_general(a, b, (dims, ((), ())), preferred_element_type=F32)


NN = ((1,), (0,))
NT = ((1,), (1,))
TN = ((0,), (0,))


def local_call(kernel, out_shape, code, *args):
    vmem = pl.BlockSpec(memory_space=pltpu.VMEM)
    return pl.pallas_call(
        kernel,
        in_specs=[pl.BlockSpec(memory_space=pltpu.SMEM)] + [vmem] * len(args),
        out_specs=jax.tree.map(lambda _: vmem, out_shape),
        out_shape=out_shape,
        compiler_params=pltpu.CompilerParams(vmem_limit_bytes=20 * 1024 * 1024),
        cost_estimate=pl.CostEstimate(flops=1000, bytes_accessed=1000, transcendentals=0),
    )(code, *args)


def shuffled(value, bit):
    half = value.shape[0] // 2
    return [(part ^ bit, value[part * half : (part + 1) * half]) for part in range(2)]


def first_kernel(product, count, code, mine, top, bottom, *refs):
    weights, (keep, away, rel) = refs[:count], refs[count:]

    def half_of_rows(step, rows):
        for place, part in shuffled(rows, code[1]):
            rel[step, place] = part
        column = 0
        for weight in weights:
            value = product(rows, weight[...])
            width = value.shape[1]
            for place, part in shuffled(value, code[1]):

                @pl.when(step == 0)
                def _():
                    keep[place, :, column : column + width] = part

                @pl.when(step == 1)
                def _():
                    away[place, :, column : column + width] = part.astype(BF)

            column += width

    @pl.loop(0, 2)
    def _(step):
        other = jnp.concatenate([top[...], bottom[...]], 0)
        half_of_rows(step, jnp.where((step ^ code[0]) == 0, mine[...], other))


def first_products(product, code, mine, other, weights, width):
    rows, quarter = mine.shape
    block = rows // 2
    return local_call(
        lambda *refs: first_kernel(product, len(weights), *refs),
        [
            jax.ShapeDtypeStruct((2, block, width), F32),
            jax.ShapeDtypeStruct((2, block, width), BF),
            jax.ShapeDtypeStruct((2, 2, block, quarter), BF),
        ],
        code,
        mine,
        *other,
        *weights,
    )


def finish(value, theirs, outs):
    half = value.shape[0] // 2
    for j in range(2):
        part = value[j * half : (j + 1) * half]
        if theirs:
            outs[0][j * half : (j + 1) * half, :] = (part + theirs[j][...].astype(F32)).astype(BF)
        else:
            outs[j][...] = part.astype(BF)


def out_rows_kernel(side, code, hidden, w_down, *refs):
    theirs, outs = refs[:2], refs[2:]
    if side == 1:
        theirs, outs = (), refs
    parts = [hidden[2 * (side ^ code[0]) + (j ^ code[1])] for j in range(2)]
    value = dot(jnp.concatenate(parts, 0), w_down[...], NN)
    finish(value, theirs, outs)


def in_rows_kernel(side, code, near, far, w_gate, w_up, *refs):
    theirs, outs = refs[:2], refs[2:]
    if side == 1:
        theirs, outs = (), refs
    place = side ^ code[0]
    value = None
    for kind, weight in ((0, w_gate), (1, w_up)):
        pair = near[2 * place + kind], far[2 * place + kind]
        parts = [jnp.where((j ^ code[1]) == 0, *pair) for j in range(2)]
        term = dot(jnp.concatenate(parts, 0), weight[...], NT)
        value = term if value is None else value + term
    finish(value, theirs, outs)


def last_products(kernel, code, pieces, weights, quarter, theirs):
    side = 1 if theirs is None else 0
    rows = pieces[0].shape[1]
    whole_shape = jax.ShapeDtypeStruct((2 * rows, quarter), BF)
    half_shape = jax.ShapeDtypeStruct((rows, quarter), BF)
    return local_call(
        lambda *refs: kernel(side, *refs),
        [half_shape] * 2 if theirs is None else whole_shape,
        code,
        *pieces,
        *weights,
        *([] if theirs is None else theirs),
    )


def slots_kernel(chips, capacity, planes, z_ref, route_mine, route_peer, local, assign, turned):
    tokens = route_mine.shape[0]
    slots = assign.shape[1]
    lanes = lax.broadcasted_iota(jnp.int32, (tokens, 128), 1)
    earlier = lax.broadcasted_iota(jnp.int32, (tokens, tokens), 0) > lax.broadcasted_iota(
        jnp.int32, (tokens, tokens), 1
    )
    places = lax.broadcasted_iota(jnp.int32, (tokens, slots), 1)
    for block, route in enumerate((route_mine, route_peer)):
        named = [route[:, k : k + 1] for k in range(2)]
        onehot = [(named[k] == lanes).astype(F32) for k in range(2)]
        before = dot(earlier.astype(BF), (onehot[0] + onehot[1]).astype(BF), NN)
        chosen = jnp.zeros((tokens, slots), F32)
        for k in range(2):
            rank = jnp.sum(before * onehot[k], axis=1, keepdims=True).astype(jnp.int32)
            expert = named[k] - z_ref[0] * chips
            inside = (expert >= 0) & (expert < chips)
            slot = jnp.where(inside, expert * (planes * capacity) + block * capacity + rank, -1)
            local[block * tokens : (block + 1) * tokens, k : k + 1] = slot
            chosen = chosen + (slot == places).astype(F32)
        assign[block * tokens : (block + 1) * tokens, :] = chosen.astype(BF)
        turned[:, block * tokens : (block + 1) * tokens] = chosen.T.astype(BF)


def rows_kernel(_, turned, mine, peer, out):
    tokens = mine.shape[0]
    rows = dot(turned[:, :tokens], mine[...], NN) + dot(turned[:, tokens:], peer[...], NN)
    out[...] = rows.astype(BF)


def picks_of(local, k, first, last, slots):
    places = lax.broadcasted_iota(jnp.int32, (last - first, slots), 1)
    return (local[first:last, k : k + 1] == places).astype(F32).astype(BF)


def cot_rows_kernel(_, local, prob, mine, peer, out):
    tokens = mine.shape[0]
    slots = out.shape[0]
    total = None
    for block, cot in enumerate((mine, peer)):
        first, last = block * tokens, (block + 1) * tokens
        value = cot[...].astype(F32)
        for k in range(2):
            scaled = (prob[first:last, k : k + 1] * value).astype(BF)
            term = dot(picks_of(local, k, first, last, slots), scaled, TN)
            total = term if total is None else total + term
    out[...] = total.astype(BF)


def combine_kernel(_, local, prob, rows, mine, peer, out_mine, out_peer, grad_p):
    tokens = mine.shape[0]
    slots = rows.shape[0]
    for block, (cot, out) in enumerate(((mine, out_mine), (peer, out_peer))):
        first, last = block * tokens, (block + 1) * tokens
        total = None
        for k in range(2):
            picked = dot(picks_of(local, k, first, last, slots), rows[...], NN)
            term = prob[first:last, k : k + 1] * picked
            total = term if total is None else total + term
            grad = jnp.sum(picked * cot[...].astype(F32), axis=1, keepdims=True)
            grad_p[first:last, k : k + 1] = grad
        out[...] = total.astype(out.dtype)


def on_device(tokens, route, probs, cotangent, gate_weight, up_weight, down_weight):
    tok_rows, quarter = tokens.shape
    top_count = route.shape[1]
    planes = lax.axis_size("z")
    chips = lax.axis_size("x") * lax.axis_size("y")
    experts = planes * chips
    capacity = 3 * tok_rows * top_count // (2 * experts)
    slots = chips * planes * capacity
    z_index = lax.axis_index("z")
    t_index = lax.axis_index("tensor")
    bit_b = t_index // 2
    bit_a = (t_index + 1) // 2 % 2
    core = lax.axis_index("core")
    code = jnp.stack(
        [jnp.where(core == 0, bit_a, bit_b), jnp.where(core == 0, bit_b, bit_a)]
    ).astype(jnp.int32)
    w_gate, w_up, w_down = gate_weight[0], up_weight[0], down_weight[0]

    route_peer, probs_peer = swap(route, "z"), swap(probs, "z")
    tok_peer = swap(tokens, "z")
    cot_peer = swap(tie(cotangent, tok_peer), "z")
    prob = jnp.concatenate([probs, probs_peer], 0)
    local, assign, turned = local_call(
        lambda *refs: slots_kernel(chips, capacity, planes, *refs),
        [
            jax.ShapeDtypeStruct((planes * tok_rows, top_count), jnp.int32),
            jax.ShapeDtypeStruct((planes * tok_rows, slots), BF),
            jax.ShapeDtypeStruct((slots, planes * tok_rows), BF),
        ],
        z_index.astype(jnp.int32)[None],
        route,
        route_peer,
    )
    rows_shape = jax.ShapeDtypeStruct((slots, quarter), BF)

    def exchange(rows):
        return lax.all_to_all(
            rows.reshape(chips, planes * capacity, quarter),
            ("x", "y"),
            split_axis=0,
            concat_axis=0,
            tiled=True,
        ).reshape(slots, quarter)

    def collect(sent):
        return sent, [swap(sent[: slots // 2], "core"), swap(sent[slots // 2 :], "core")]

    tok_sent = exchange(local_call(rows_kernel, rows_shape, code, turned, tokens, tok_peer))
    cot_rows = local_call(cot_rows_kernel, rows_shape, code, local, prob, cotangent, cot_peer)
    cot_sent = exchange(tie(cot_rows, tok_sent))
    in_mine, in_other = collect(tie(tok_sent, cot_rows))
    half = w_gate.shape[1]

    def nn(rows, weight):
        return dot(rows, weight, NN)

    def nt(rows, weight):
        return dot(rows, weight, NT)

    keep, away, rows_in = first_products(nn, code, in_mine, in_other, (w_gate, w_up), 2 * half)
    got = cross(away, FIRST)
    cot_mine, cot_other = collect(tie(cot_sent, away))
    keep_c, away_c, rows_cot = first_products(nt, code, cot_mine, cot_other, (w_down,), half)
    got_c = cross(away_c, FIRST)
    gate_up = keep + tie(got, away_c).astype(F32)
    got = cross(gate_up[1].astype(BF), SECOND)

    gate_up = gate_up[0] + got.astype(F32)
    gate, up = gate_up[:, :half], gate_up[:, half:]
    hidden = (jax.nn.silu(gate) * up).astype(BF)

    hidden_cot = keep_c + got_c.astype(F32)
    hidden = jnp.stack([hidden, cross(hidden, FIRST)])
    got = cross(hidden_cot[1].astype(BF), SECOND)
    hidden_cot = hidden_cot[0] + got.astype(F32)
    sig = jax.nn.sigmoid(gate)
    gate_cot = (hidden_cot * up * sig * (1.0 + gate * (1.0 - sig))).astype(BF)
    up_cot = (hidden_cot * gate * sig).astype(BF)

    own = jnp.stack([gate_cot, up_cot])
    got = cross(hidden, SECOND)
    hidden = jnp.stack([hidden[0], got[0], hidden[1], got[1]])
    got = cross(own, FIRST)

    def send_back(kernel, pieces, weights, after=None):
        away = last_products(kernel, code, pieces, weights, quarter, None)
        theirs = [swap(part, "core") for part in away]
        if after is not None:
            theirs = tie(theirs, after)
        return last_products(kernel, code, pieces, weights, quarter, theirs)

    out_back = send_back(out_rows_kernel, (hidden,), (w_down,))
    returned = exchange(out_back)
    near = jnp.concatenate([own, got], 0)
    far = cross(near, SECOND)
    hidden, rows_cot = tie((hidden, rows_cot), out_back)
    grad_down = dot(hidden.reshape(2 * slots, half), rows_cot.reshape(2 * slots, quarter), TN).astype(BF)
    out_mine, out_peer, grad_p = local_call(
        combine_kernel,
        [
            jax.ShapeDtypeStruct((tok_rows, quarter), F32),
            jax.ShapeDtypeStruct((tok_rows, quarter), BF),
            jax.ShapeDtypeStruct((planes * tok_rows, top_count), F32),
        ],
        code,
        local,
        prob,
        returned,
        cotangent,
        cot_peer,
    )
    in_back = send_back(in_rows_kernel, (near, far), (w_gate, w_up), grad_down)
    returned_in = exchange(in_back)
    near, far, out_mine, grad_p = tie((near, far, out_mine, grad_p), in_back)

    moe_out = (out_mine + swap(out_peer, "z").astype(F32)).astype(BF)
    grad_p = grad_p.T
    grad_p = grad_p[:, :tok_rows] + swap(grad_p[:, tok_rows:], "z")
    grad_p = grad_p + cross(grad_p, FIRST)
    grad_p = grad_p + cross(grad_p, SECOND)

    tok_part = dot(assign, returned_in, NN)
    grad_tokens = (tok_part[:tok_rows] + swap(tok_part[tok_rows:].astype(BF), "z").astype(F32)).astype(BF)

    rows_in = rows_in.reshape(2 * slots, quarter)

    def all_rows(kind):
        parts = [near[kind], far[kind], near[2 + kind], far[2 + kind]]
        return jnp.concatenate(parts, 0)

    grad_gate = dot(rows_in, all_rows(0), TN).astype(BF)
    grad_up = dot(rows_in, all_rows(1), TN).astype(BF)
    return (moe_out, grad_p.T, grad_tokens, grad_gate[None], grad_up[None], grad_down[None])


def solution(mesh):
    lanes = ("z", "x", "y", "core")
    fine = Mesh(mesh.devices.reshape(2, 4, 4, 2, 4), lanes + ("tensor",))
    placed = (
        P(lanes, "tensor"),
        P(lanes, None),
        P(lanes, None),
        P(lanes, "tensor"),
        P(lanes, "tensor", None),
        P(lanes, "tensor", None),
        P(lanes, None, "tensor"),
    )
    return jax.shard_map(
        on_device,
        mesh=fine,
        in_specs=placed,
        out_specs=(
            P(lanes, "tensor"),
            P(lanes, None),
            P(lanes, "tensor"),
            P(lanes, "tensor", None),
            P(lanes, "tensor", None),
            P(lanes, None, "tensor"),
        ),
        check_vma=False,
    )
```

```python
import jax
import jax.numpy as jnp
from jax import lax
from jax.experimental import pallas as pl
from jax.experimental.pallas import tpu as pltpu
from jax.sharding import Mesh, PartitionSpec as P

BF = jnp.bfloat16
F32 = jnp.float32
PAIR = [(0, 1), (1, 0)]
EDGE_A = [(0, 1), (1, 0), (2, 3), (3, 2)]
EDGE_B = [(0, 3), (3, 0), (1, 2), (2, 1)]


def swap(value, axis):
    return lax.ppermute(value, axis, PAIR)


FIRST = [(i, j) for i, j in EDGE_A] + [(4 + i, 4 + j) for i, j in EDGE_B]
SECOND = [(i, j) for i, j in EDGE_B] + [(4 + i, 4 + j) for i, j in EDGE_A]


def cross(value, step):
    return lax.ppermute(value, ("core", "tensor"), step)


def tie(value, after):
    return lax.optimization_barrier((value, after))[0]


def dot(a, b, dims):
    return lax.dot_general(a, b, (dims, ((), ())), preferred_element_type=F32)


NN = ((1,), (0,))
NT = ((1,), (1,))
TN = ((0,), (0,))


def local_call(kernel, out_shape, code, *args):
    vmem = pl.BlockSpec(memory_space=pltpu.VMEM)
    return pl.pallas_call(
        kernel,
        in_specs=[pl.BlockSpec(memory_space=pltpu.SMEM)] + [vmem] * len(args),
        out_specs=jax.tree.map(lambda _: vmem, out_shape),
        out_shape=out_shape,
        compiler_params=pltpu.CompilerParams(vmem_limit_bytes=20 * 1024 * 1024),
        cost_estimate=pl.CostEstimate(flops=1000, bytes_accessed=1000, transcendentals=0),
    )(code, *args)


def first_kernel(product, count, code, mine, top, bottom, *refs):
    weights, (keep, away, rel) = refs[:count], refs[count:]
    block, quarter = top.shape

    @pl.loop(0, 2)
    def _(step):
        @pl.when(step == code[0])
        def _():
            for part in range(2):
                rel[step, part ^ code[1]] = mine[part * block : (part + 1) * block, :]

        @pl.when(step != code[0])
        def _():
            for part, rows in enumerate((top, bottom)):
                rel[step, part ^ code[1]] = rows[...]

        column = 0
        for weight in weights:
            value = product(rel[step].reshape(2 * block, quarter), weight[...])
            width = value.shape[1]
            value = value.reshape(2, block, width)

            @pl.when(step == 0)
            def _():
                keep[:, :, column : column + width] = value

            @pl.when(step == 1)
            def _():
                away[:, :, column : column + width] = value.astype(BF)

            column += width


def first_products(product, code, mine, other, weights, width):
    rows, quarter = mine.shape
    block = rows // 2
    return local_call(
        lambda *refs: first_kernel(product, len(weights), *refs),
        [
            jax.ShapeDtypeStruct((2, block, width), F32),
            jax.ShapeDtypeStruct((2, block, width), BF),
            jax.ShapeDtypeStruct((2, 2, block, quarter), BF),
        ],
        code,
        mine,
        *other,
        *weights,
    )


def finish(value, theirs, outs):
    half = value.shape[0] // 2
    for j in range(2):
        part = value[j * half : (j + 1) * half]
        if len(outs) == 1 and not theirs:
            outs[0][j * half : (j + 1) * half, :] = part
        elif theirs:
            outs[0][j * half : (j + 1) * half, :] = (part + theirs[j][...].astype(F32)).astype(BF)
        else:
            outs[j][...] = part.astype(BF)


def add_kernel(_, mine, top, bottom, out):
    half = top.shape[0]
    out[:half, :] = (mine[:half, :] + top[...].astype(F32)).astype(BF)
    out[half:, :] = (mine[half:, :] + bottom[...].astype(F32)).astype(BF)


def out_rows_kernel(side, code, hidden, w_down, *refs):
    theirs, outs = refs[:-1], refs[-1:]
    if side == 1:
        theirs, outs = (), refs
    parts = [hidden[2 * (side ^ code[0]) + (j ^ code[1])] for j in range(2)]
    value = dot(jnp.concatenate(parts, 0), w_down[...], NN)
    finish(value, theirs, outs)


def in_rows_kernel(side, code, near, far, w_gate, w_up, *refs):
    theirs, outs = refs[:-1], refs[-1:]
    if side == 1:
        theirs, outs = (), refs
    place = side ^ code[0]
    value = None
    for kind, weight in ((0, w_gate), (1, w_up)):
        pair = near[2 * place + kind], far[2 * place + kind]
        parts = [jnp.where((j ^ code[1]) == 0, *pair) for j in range(2)]
        term = dot(jnp.concatenate(parts, 0), weight[...], NT)
        value = term if value is None else value + term
    finish(value, theirs, outs)


def last_products(kernel, code, pieces, weights, quarter, theirs):
    side = 1 if theirs is None else 0
    rows = pieces[0].shape[1]
    whole_shape = jax.ShapeDtypeStruct((2 * rows, quarter), BF if theirs else F32)
    half_shape = jax.ShapeDtypeStruct((rows, quarter), BF)
    return local_call(
        lambda *refs: kernel(side, *refs),
        [half_shape] * 2 if theirs is None else whole_shape,
        code,
        *pieces,
        *weights,
        *([] if theirs is None else theirs),
    )


def slots_kernel(chips, capacity, planes, z_ref, route_mine, route_peer, local, assign, turned):
    tokens = route_mine.shape[0]
    slots = assign.shape[1]
    lanes = lax.broadcasted_iota(jnp.int32, (tokens, 128), 1)
    earlier = lax.broadcasted_iota(jnp.int32, (tokens, tokens), 0) > lax.broadcasted_iota(
        jnp.int32, (tokens, tokens), 1
    )
    places = lax.broadcasted_iota(jnp.int32, (tokens, slots), 1)
    for block, route in enumerate((route_mine, route_peer)):
        named = [route[:, k : k + 1] for k in range(2)]
        onehot = [(named[k] == lanes).astype(F32) for k in range(2)]
        before = dot(earlier.astype(BF), (onehot[0] + onehot[1]).astype(BF), NN)
        chosen = jnp.zeros((tokens, slots), F32)
        for k in range(2):
            rank = jnp.sum(before * onehot[k], axis=1, keepdims=True).astype(jnp.int32)
            expert = named[k] - z_ref[0] * chips
            inside = (expert >= 0) & (expert < chips)
            slot = jnp.where(inside, expert * (planes * capacity) + block * capacity + rank, -1)
            local[block * tokens : (block + 1) * tokens, k : k + 1] = slot
            chosen = chosen + (slot == places).astype(F32)
        assign[block * tokens : (block + 1) * tokens, :] = chosen.astype(BF)
        turned[:, block * tokens : (block + 1) * tokens] = chosen.T.astype(BF)


def rows_kernel(_, turned, mine, peer, out):
    every = jnp.concatenate([mine[...], peer[...]], 0)
    width = min(256, every.shape[1])
    for at in range(0, every.shape[1], width):
        out[:, at : at + width] = dot(turned[...], every[:, at : at + width], NN).astype(BF)


def picks_of(local, k, first, last, slots):
    places = lax.broadcasted_iota(jnp.int32, (last - first, slots), 1)
    return (local[first:last, k : k + 1] == places).astype(F32).astype(BF)


def cot_rows_kernel(_, local, prob, mine, peer, out):
    tokens = mine.shape[0]
    slots = out.shape[0]
    total = None
    for block, cot in enumerate((mine, peer)):
        first, last = block * tokens, (block + 1) * tokens
        value = cot[...].astype(F32)
        for k in range(2):
            scaled = (prob[first:last, k : k + 1] * value).astype(BF)
            term = dot(picks_of(local, k, first, last, slots), scaled, TN)
            total = term if total is None else total + term
    out[...] = total.astype(BF)


def combine_kernel(_, local, prob, rows, mine, peer, out_mine, out_peer, grad_p):
    tokens = mine.shape[0]
    slots = rows.shape[0]
    for block, (cot, out) in enumerate(((mine, out_mine), (peer, out_peer))):
        first, last = block * tokens, (block + 1) * tokens
        total = None
        for k in range(2):
            picked = dot(picks_of(local, k, first, last, slots), rows[...], NN)
            term = prob[first:last, k : k + 1] * picked
            total = term if total is None else total + term
            grad = jnp.sum(picked * cot[...].astype(F32), axis=1, keepdims=True)
            grad_p[first:last, k : k + 1] = grad
        out[...] = total.astype(out.dtype)


def on_device(tokens, route, probs, cotangent, gate_weight, up_weight, down_weight):
    tok_rows, quarter = tokens.shape
    top_count = route.shape[1]
    planes = lax.axis_size("z")
    chips = lax.axis_size("x") * lax.axis_size("y")
    experts = planes * chips
    capacity = 3 * tok_rows * top_count // (2 * experts)
    slots = chips * planes * capacity
    z_index = lax.axis_index("z")
    t_index = lax.axis_index("tensor")
    bit_b = t_index // 2
    bit_a = (t_index + 1) // 2 % 2
    core = lax.axis_index("core")
    code = jnp.stack(
        [jnp.where(core == 0, bit_a, bit_b), jnp.where(core == 0, bit_b, bit_a)]
    ).astype(jnp.int32)
    w_gate, w_up, w_down = gate_weight[0], up_weight[0], down_weight[0]

    route_peer, probs_peer = swap(route, "z"), swap(probs, "z")
    tok_peer = swap(tokens, "z")
    cot_peer = swap(tie(cotangent, tok_peer), "z")
    prob = jnp.concatenate([probs, probs_peer], 0)
    local, assign, turned = local_call(
        lambda *refs: slots_kernel(chips, capacity, planes, *refs),
        [
            jax.ShapeDtypeStruct((planes * tok_rows, top_count), jnp.int32),
            jax.ShapeDtypeStruct((planes * tok_rows, slots), BF),
            jax.ShapeDtypeStruct((slots, planes * tok_rows), BF),
        ],
        z_index.astype(jnp.int32)[None],
        route,
        route_peer,
    )
    rows_shape = jax.ShapeDtypeStruct((slots, quarter), BF)

    def exchange(rows):
        return lax.all_to_all(
            rows.reshape(chips, planes * capacity, quarter),
            ("x", "y"),
            split_axis=0,
            concat_axis=0,
            tiled=True,
        ).reshape(slots, quarter)

    def collect(sent):
        return sent, [swap(sent[: slots // 2], "core"), swap(sent[slots // 2 :], "core")]

    tok_sent = exchange(local_call(rows_kernel, rows_shape, code, turned, tokens, tok_peer))
    cot_rows = local_call(cot_rows_kernel, rows_shape, code, local, prob, cotangent, cot_peer)
    cot_sent = exchange(tie(cot_rows, tok_sent))
    in_mine, in_other = collect(tie(tok_sent, cot_rows))
    half = w_gate.shape[1]

    def nn(rows, weight):
        return dot(rows, weight, NN)

    def nt(rows, weight):
        return dot(rows, weight, NT)

    keep, away, rows_in = first_products(nn, code, in_mine, in_other, (w_gate, w_up), 2 * half)
    got = cross(away, FIRST)
    cot_mine, cot_other = collect(tie(cot_sent, away))
    keep_c, away_c, rows_cot = first_products(nt, code, cot_mine, cot_other, (w_down,), half)
    got_c = cross(away_c, FIRST)
    gate_up = keep + tie(got, away_c).astype(F32)
    got = cross(gate_up[1].astype(BF), SECOND)

    hidden_cot = keep_c + got_c.astype(F32)
    away_c = hidden_cot[1].astype(BF)
    gate_up = gate_up[0] + tie(got, away_c).astype(F32)
    gate, up = gate_up[:, :half], gate_up[:, half:]
    hidden = (jax.nn.silu(gate) * up).astype(BF)

    got_h = cross(hidden, FIRST)
    got = cross(away_c, SECOND)
    got, got_h = lax.optimization_barrier((got, got_h))
    hidden = jnp.stack([hidden, got_h])
    hidden_cot = hidden_cot[0] + got.astype(F32)
    sig = jax.nn.sigmoid(gate)
    gate_cot = (hidden_cot * up * sig * (1.0 + gate * (1.0 - sig))).astype(BF)
    up_cot = (hidden_cot * gate * sig).astype(BF)

    own = jnp.stack([gate_cot, up_cot])
    got = cross(hidden, SECOND)
    hidden = jnp.stack([hidden[0], got[0], hidden[1], got[1]])
    got = cross(own, FIRST)

    def send_back(kernel, pieces, weights, after=None):
        away = last_products(kernel, code, pieces, weights, quarter, None)
        theirs = [swap(part, "core") for part in away]
        if after is not None:
            theirs = tie(theirs, after)
        return last_products(kernel, code, pieces, weights, quarter, theirs)

    out_back = send_back(out_rows_kernel, (hidden,), (w_down,))
    returned = exchange(out_back)
    near = jnp.concatenate([own, got], 0)
    far = cross(near, SECOND)
    hidden, rows_cot = tie((hidden, rows_cot), out_back)
    grad_down = dot(hidden.reshape(2 * slots, half), rows_cot.reshape(2 * slots, quarter), TN).astype(BF)
    out_mine, out_peer, grad_p = local_call(
        combine_kernel,
        [
            jax.ShapeDtypeStruct((tok_rows, quarter), F32),
            jax.ShapeDtypeStruct((tok_rows, quarter), BF),
            jax.ShapeDtypeStruct((planes * tok_rows, top_count), F32),
        ],
        code,
        local,
        prob,
        returned,
        cotangent,
        cot_peer,
    )
    far = tie(far, grad_down)
    away_in = last_products(in_rows_kernel, code, (near, far), (w_gate, w_up), quarter, None)
    theirs_in = [swap(part, "core") for part in away_in]
    mine_in = last_products(in_rows_kernel, code, (near, far), (w_gate, w_up), quarter, ())
    in_back = local_call(
        add_kernel, jax.ShapeDtypeStruct((slots, quarter), BF), code, mine_in, *tie(theirs_in, mine_in)
    )
    returned_in = exchange(in_back)
    near, far, out_mine, grad_p = tie((near, far, out_mine, grad_p), in_back)

    out_theirs = swap(out_peer, "z")
    moe_out = (out_mine + out_theirs.astype(F32)).astype(BF)
    rows_in = rows_in.reshape(2 * slots, quarter)

    def all_rows(kind):
        parts = [near[kind], far[kind], near[2 + kind], far[2 + kind]]
        return jnp.concatenate(parts, 0)

    grad_gate = dot(rows_in, all_rows(0), TN).astype(BF)
    grad_up = dot(rows_in, all_rows(1), TN).astype(BF)
    grad_p = grad_p.T
    theirs = tie(swap(grad_p[:, tok_rows:], "z"), (grad_gate, grad_up))
    grad_p = grad_p[:, :tok_rows] + theirs
    grad_p = tie(grad_p + cross(grad_p, FIRST), out_theirs)
    grad_p = grad_p + cross(grad_p, SECOND)

    tok_part = dot(assign, returned_in, NN)
    grad_tokens = (tok_part[:tok_rows] + swap(tok_part[tok_rows:].astype(BF), "z").astype(F32)).astype(BF)

    return (moe_out, grad_p.T, grad_tokens, grad_gate[None], grad_up[None], grad_down[None])


def solution(mesh):
    lanes = ("z", "x", "y", "core")
    fine = Mesh(mesh.devices.reshape(2, 4, 4, 2, 4), lanes + ("tensor",))
    placed = (
        P(lanes, "tensor"),
        P(lanes, None),
        P(lanes, None),
        P(lanes, "tensor"),
        P(lanes, "tensor", None),
        P(lanes, "tensor", None),
        P(lanes, None, "tensor"),
    )
    return jax.shard_map(
        on_device,
        mesh=fine,
        in_specs=placed,
        out_specs=(
            P(lanes, "tensor"),
            P(lanes, None),
            P(lanes, "tensor"),
            P(lanes, "tensor", None),
            P(lanes, "tensor", None),
            P(lanes, None, "tensor"),
        ),
        check_vma=False,
    )
```

```python
import jax
import jax.numpy as jnp
from jax import lax
from jax.experimental import pallas as pl
from jax.experimental.pallas import tpu as pltpu
from jax.sharding import Mesh, PartitionSpec as P

BF = jnp.bfloat16
F32 = jnp.float32
PAIR = [(0, 1), (1, 0)]
EDGE_A = [(0, 1), (1, 0), (2, 3), (3, 2)]
EDGE_B = [(0, 3), (3, 0), (1, 2), (2, 1)]


def swap(value, axis):
    return lax.ppermute(value, axis, PAIR)


FIRST = [(i, j) for i, j in EDGE_A] + [(4 + i, 4 + j) for i, j in EDGE_B]
SECOND = [(i, j) for i, j in EDGE_B] + [(4 + i, 4 + j) for i, j in EDGE_A]


def cross(value, step):
    return lax.ppermute(value, ("core", "tensor"), step)


def tie(value, after):
    return lax.optimization_barrier((value, after))[0]


def dot(a, b, dims):
    return lax.dot_general(a, b, (dims, ((), ())), preferred_element_type=F32)


NN = ((1,), (0,))
NT = ((1,), (1,))
TN = ((0,), (0,))


def local_call(kernel, out_shape, code, *args):
    vmem = pl.BlockSpec(memory_space=pltpu.VMEM)
    return pl.pallas_call(
        kernel,
        in_specs=[pl.BlockSpec(memory_space=pltpu.SMEM)] + [vmem] * len(args),
        out_specs=jax.tree.map(lambda _: vmem, out_shape),
        out_shape=out_shape,
        compiler_params=pltpu.CompilerParams(vmem_limit_bytes=20 * 1024 * 1024),
        cost_estimate=pl.CostEstimate(flops=1000, bytes_accessed=1000, transcendentals=0),
    )(code, *args)


def first_kernel(product, count, code, mine, top, bottom, *refs):
    weights, (keep, away, rel) = refs[:count], refs[count:]
    block, quarter = top.shape

    @pl.loop(0, 2)
    def _(step):
        @pl.when(step == code[0])
        def _():
            for part in range(2):
                rel[step, part ^ code[1]] = mine[part * block : (part + 1) * block, :]

        @pl.when(step != code[0])
        def _():
            for part, rows in enumerate((top, bottom)):
                rel[step, part ^ code[1]] = rows[...]

        column = 0
        for weight in weights:
            value = product(rel[step].reshape(2 * block, quarter), weight[...])
            width = value.shape[1]
            value = value.reshape(2, block, width)

            @pl.when(step == 0)
            def _():
                keep[:, :, column : column + width] = value

            @pl.when(step == 1)
            def _():
                away[:, :, column : column + width] = value.astype(BF)

            column += width


def first_products(product, code, mine, other, weights, width):
    rows, quarter = mine.shape
    block = rows // 2
    return local_call(
        lambda *refs: first_kernel(product, len(weights), *refs),
        [
            jax.ShapeDtypeStruct((2, block, width), F32),
            jax.ShapeDtypeStruct((2, block, width), BF),
            jax.ShapeDtypeStruct((2, 2, block, quarter), BF),
        ],
        code,
        mine,
        *other,
        *weights,
    )


def finish(value, theirs, outs):
    half = value.shape[0] // 2
    for j in range(2):
        part = value[j * half : (j + 1) * half]
        if len(outs) == 1 and not theirs:
            outs[0][j * half : (j + 1) * half, :] = part
        elif theirs:
            outs[0][j * half : (j + 1) * half, :] = (part + theirs[j][...].astype(F32)).astype(BF)
        else:
            outs[j][...] = part.astype(BF)


def add_kernel(_, mine, top, bottom, out):
    half = top.shape[0]
    out[:half, :] = (mine[:half, :] + top[...].astype(F32)).astype(BF)
    out[half:, :] = (mine[half:, :] + bottom[...].astype(F32)).astype(BF)


def out_rows_kernel(side, code, hidden, w_down, *refs):
    theirs, outs = refs[:-1], refs[-1:]
    if side == 1:
        theirs, outs = (), refs
    parts = [hidden[2 * (side ^ code[0]) + (j ^ code[1])] for j in range(2)]
    value = dot(jnp.concatenate(parts, 0), w_down[...], NN)
    finish(value, theirs, outs)


def in_rows_kernel(side, code, near, far, w_gate, w_up, *refs):
    theirs, outs = refs[:-1], refs[-1:]
    if side == 1:
        theirs, outs = (), refs
    place = side ^ code[0]
    value = None
    for kind, weight in ((0, w_gate), (1, w_up)):
        pair = near[2 * place + kind], far[2 * place + kind]
        parts = [jnp.where((j ^ code[1]) == 0, *pair) for j in range(2)]
        term = dot(jnp.concatenate(parts, 0), weight[...], NT)
        value = term if value is None else value + term
    finish(value, theirs, outs)


def last_products(kernel, code, pieces, weights, quarter, theirs):
    side = 1 if theirs is None else 0
    rows = pieces[0].shape[1]
    whole_shape = jax.ShapeDtypeStruct((2 * rows, quarter), BF if theirs else F32)
    half_shape = jax.ShapeDtypeStruct((rows, quarter), BF)
    return local_call(
        lambda *refs: kernel(side, *refs),
        [half_shape] * 2 if theirs is None else whole_shape,
        code,
        *pieces,
        *weights,
        *([] if theirs is None else theirs),
    )


def slots_kernel(chips, capacity, planes, z_ref, route_mine, route_peer, local, assign, turned):
    tokens = route_mine.shape[0]
    slots = assign.shape[1]
    lanes = lax.broadcasted_iota(jnp.int32, (tokens, 128), 1)
    earlier = lax.broadcasted_iota(jnp.int32, (tokens, tokens), 0) > lax.broadcasted_iota(
        jnp.int32, (tokens, tokens), 1
    )
    places = lax.broadcasted_iota(jnp.int32, (tokens, slots), 1)
    for block, route in enumerate((route_mine, route_peer)):
        named = [route[:, k : k + 1] for k in range(2)]
        onehot = [(named[k] == lanes).astype(F32) for k in range(2)]
        before = dot(earlier.astype(BF), (onehot[0] + onehot[1]).astype(BF), NN)
        chosen = jnp.zeros((tokens, slots), F32)
        for k in range(2):
            rank = jnp.sum(before * onehot[k], axis=1, keepdims=True).astype(jnp.int32)
            expert = named[k] - z_ref[0] * chips
            inside = (expert >= 0) & (expert < chips)
            slot = jnp.where(inside, expert * (planes * capacity) + block * capacity + rank, -1)
            local[block * tokens : (block + 1) * tokens, k : k + 1] = slot
            chosen = chosen + (slot == places).astype(F32)
        assign[block * tokens : (block + 1) * tokens, :] = chosen.astype(BF)
        turned[:, block * tokens : (block + 1) * tokens] = chosen.T.astype(BF)


def rows_kernel(_, turned, mine, peer, out):
    every = jnp.concatenate([mine[...], peer[...]], 0)
    width = min(256, every.shape[1])
    for at in range(0, every.shape[1], width):
        out[:, at : at + width] = dot(turned[...], every[:, at : at + width], NN).astype(BF)


def picks_of(local, k, first, last, slots):
    places = lax.broadcasted_iota(jnp.int32, (last - first, slots), 1)
    return (local[first:last, k : k + 1] == places).astype(F32).astype(BF)


def cot_rows_kernel(_, local, prob, mine, peer, out):
    tokens = mine.shape[0]
    slots = out.shape[0]
    total = None
    for block, cot in enumerate((mine, peer)):
        first, last = block * tokens, (block + 1) * tokens
        value = cot[...].astype(F32)
        for k in range(2):
            scaled = (prob[first:last, k : k + 1] * value).astype(BF)
            term = dot(picks_of(local, k, first, last, slots), scaled, TN)
            total = term if total is None else total + term
    out[...] = total.astype(BF)


def combine_kernel(_, local, prob, rows, mine, peer, out_mine, out_peer, grad_p):
    tokens = mine.shape[0]
    slots = rows.shape[0]
    for block, (cot, out) in enumerate(((mine, out_mine), (peer, out_peer))):
        first, last = block * tokens, (block + 1) * tokens
        total = None
        for k in range(2):
            picked = dot(picks_of(local, k, first, last, slots), rows[...], NN)
            term = prob[first:last, k : k + 1] * picked
            total = term if total is None else total + term
            grad = jnp.sum(picked * cot[...].astype(F32), axis=1, keepdims=True)
            grad_p[first:last, k : k + 1] = grad
        out[...] = total.astype(out.dtype)


def on_device(tokens, route, probs, cotangent, gate_weight, up_weight, down_weight):
    tok_rows, quarter = tokens.shape
    top_count = route.shape[1]
    planes = lax.axis_size("z")
    chips = lax.axis_size("x") * lax.axis_size("y")
    experts = planes * chips
    capacity = 3 * tok_rows * top_count // (2 * experts)
    slots = chips * planes * capacity
    z_index = lax.axis_index("z")
    t_index = lax.axis_index("tensor")
    bit_b = t_index // 2
    bit_a = (t_index + 1) // 2 % 2
    core = lax.axis_index("core")
    code = jnp.stack(
        [jnp.where(core == 0, bit_a, bit_b), jnp.where(core == 0, bit_b, bit_a)]
    ).astype(jnp.int32)
    w_gate, w_up, w_down = gate_weight[0], up_weight[0], down_weight[0]

    route_peer, probs_peer = swap(route, "z"), swap(probs, "z")
    tok_peer = swap(tokens, "z")
    cot_peer = swap(tie(cotangent, tok_peer), "z")
    prob = jnp.concatenate([probs, probs_peer], 0)
    local, assign, turned = local_call(
        lambda *refs: slots_kernel(chips, capacity, planes, *refs),
        [
            jax.ShapeDtypeStruct((planes * tok_rows, top_count), jnp.int32),
            jax.ShapeDtypeStruct((planes * tok_rows, slots), BF),
            jax.ShapeDtypeStruct((slots, planes * tok_rows), BF),
        ],
        z_index.astype(jnp.int32)[None],
        route,
        route_peer,
    )
    rows_shape = jax.ShapeDtypeStruct((slots, quarter), BF)

    def exchange(rows):
        return lax.all_to_all(
            rows.reshape(chips, planes * capacity, quarter),
            ("x", "y"),
            split_axis=0,
            concat_axis=0,
            tiled=True,
        ).reshape(slots, quarter)

    def collect(sent):
        return sent, [swap(sent[: slots // 2], "core"), swap(sent[slots // 2 :], "core")]

    tok_sent = exchange(local_call(rows_kernel, rows_shape, code, turned, tokens, tok_peer))
    cot_rows = local_call(cot_rows_kernel, rows_shape, code, local, prob, cotangent, cot_peer)
    cot_sent = exchange(tie(cot_rows, tok_sent))
    in_mine, in_other = collect(tie(tok_sent, cot_rows))
    half = w_gate.shape[1]

    def nn(rows, weight):
        return dot(rows, weight, NN)

    def nt(rows, weight):
        return dot(rows, weight, NT)

    keep, away, rows_in = first_products(nn, code, in_mine, in_other, (w_gate, w_up), 2 * half)
    got = cross(away, FIRST)
    cot_mine, cot_other = collect(tie(cot_sent, away))
    keep_c, away_c, rows_cot = first_products(nt, code, cot_mine, cot_other, (w_down,), half)
    got_c = cross(away_c, FIRST)
    gate_up = keep + tie(got, away_c).astype(F32)
    got = cross(gate_up[1].astype(BF), SECOND)

    hidden_cot = keep_c + got_c.astype(F32)
    away_c = hidden_cot[1].astype(BF)
    gate_up = gate_up[0] + tie(got, away_c).astype(F32)
    gate, up = gate_up[:, :half], gate_up[:, half:]
    hidden = (jax.nn.silu(gate) * up).astype(BF)

    got_h = cross(hidden, FIRST)
    got = cross(away_c, SECOND)
    got, got_h = lax.optimization_barrier((got, got_h))
    hidden = jnp.stack([hidden, got_h])
    hidden_cot = hidden_cot[0] + got.astype(F32)
    sig = jax.nn.sigmoid(gate)
    gate_cot = (hidden_cot * up * sig * (1.0 + gate * (1.0 - sig))).astype(BF)
    up_cot = (hidden_cot * gate * sig).astype(BF)

    own = jnp.stack([gate_cot, up_cot])
    got = cross(hidden, SECOND)
    hidden = jnp.stack([hidden[0], got[0], hidden[1], got[1]])
    got = cross(own, FIRST)

    def send_back(kernel, pieces, weights, after=None):
        away = last_products(kernel, code, pieces, weights, quarter, None)
        theirs = [swap(part, "core") for part in away]
        if after is not None:
            theirs = tie(theirs, after)
        return last_products(kernel, code, pieces, weights, quarter, theirs)

    out_back = send_back(out_rows_kernel, (hidden,), (w_down,))
    returned = exchange(out_back)
    near = jnp.concatenate([own, got], 0)
    far = cross(near, SECOND)
    hidden, rows_cot = tie((hidden, rows_cot), out_back)
    grad_down = dot(hidden.reshape(2 * slots, half), rows_cot.reshape(2 * slots, quarter), TN).astype(BF)
    out_mine, out_peer, grad_p = local_call(
        combine_kernel,
        [
            jax.ShapeDtypeStruct((tok_rows, quarter), F32),
            jax.ShapeDtypeStruct((tok_rows, quarter), BF),
            jax.ShapeDtypeStruct((planes * tok_rows, top_count), F32),
        ],
        code,
        local,
        prob,
        returned,
        cotangent,
        cot_peer,
    )
    far = tie(far, grad_down)
    away_in = last_products(in_rows_kernel, code, (near, far), (w_gate, w_up), quarter, None)
    theirs_in = [swap(part, "core") for part in away_in]
    mine_in = last_products(in_rows_kernel, code, (near, far), (w_gate, w_up), quarter, ())
    in_back = local_call(
        add_kernel, jax.ShapeDtypeStruct((slots, quarter), BF), code, mine_in, *tie(theirs_in, mine_in)
    )
    returned_in = exchange(in_back)
    near, far, out_mine, grad_p = tie((near, far, out_mine, grad_p), in_back)

    out_theirs = swap(out_peer, "z")
    moe_out = (out_mine + out_theirs.astype(F32)).astype(BF)
    rows_in = rows_in.reshape(2 * slots, quarter)

    def all_rows(kind):
        parts = [near[kind], far[kind], near[2 + kind], far[2 + kind]]
        return jnp.concatenate(parts, 0)

    grad_gate = dot(rows_in, all_rows(0), TN).astype(BF)
    grad_up = dot(rows_in, all_rows(1), TN).astype(BF)
    grad_p = grad_p.T
    theirs = tie(swap(grad_p[:, tok_rows:], "z"), (grad_gate, grad_up))
    grad_p = grad_p[:, :tok_rows] + theirs
    grad_p = tie(grad_p, out_theirs)
    got_p = cross(grad_p, FIRST)

    tok_part = dot(assign, returned_in, NN)
    tok_away = tok_part[tok_rows:].astype(BF)
    grad_tokens = (tok_part[:tok_rows] + swap(tok_away, "z").astype(F32)).astype(BF)
    grad_p = grad_p + tie(got_p, tok_away)
    grad_p = grad_p + cross(grad_p, SECOND)
    return (moe_out, grad_p.T, grad_tokens, grad_gate[None], grad_up[None], grad_down[None])


def solution(mesh):
    lanes = ("z", "x", "y", "core")
    fine = Mesh(mesh.devices.reshape(2, 4, 4, 2, 4), lanes + ("tensor",))
    placed = (
        P(lanes, "tensor"),
        P(lanes, None),
        P(lanes, None),
        P(lanes, "tensor"),
        P(lanes, "tensor", None),
        P(lanes, "tensor", None),
        P(lanes, None, "tensor"),
    )
    return jax.shard_map(
        on_device,
        mesh=fine,
        in_specs=placed,
        out_specs=(
            P(lanes, "tensor"),
            P(lanes, None),
            P(lanes, "tensor"),
            P(lanes, "tensor", None),
            P(lanes, "tensor", None),
            P(lanes, None, "tensor"),
        ),
        check_vma=False,
    )
```
